32 devices in a mesh: fsdp: 16 (over z, x, core), seq: 2 (over y).
Axes of the slice: x: 2, y: 2, z: 4, core: 2. Of those that a mesh axis runs over, the one named last changes fastest.
Arguments:
- tokens: bfloat16 [16, 1024, 1024], P('fsdp', 'seq'), may hold values from -6 to 6
- cotangent: bfloat16 [16, 1024, 1024], P('fsdp', 'seq'), may hold values from -6 to 6
- doc_start: int32 [16, 1024], P('fsdp', 'seq'), may hold values from 0 to 1023, as said below
- w_in: bfloat16 [1024, 4096], P('fsdp', 'seq'), may hold values from -0.1875 to 0.1875
- w_dt: bfloat16 [1024, 24], P('fsdp'), may hold values from -0.1875 to 0.1875
- w_out: bfloat16 [2048, 1024], P('fsdp', 'seq'), may hold values from -0.1875 to 0.1875
- w_gate_up: bfloat16 [1024, 4096], P('fsdp', 'seq'), may hold values from -0.1875 to 0.1875
- w_down: bfloat16 [2048, 1024], P('fsdp', 'seq'), may hold values from -0.125 to 0.125
- norm_gains: float32 [2, 1024], replicated, may hold values from 0.5 to 1.5
- conv_params: float32 [5, 1792], replicated, may hold values from -0.5 to 0.5
- ssm_gain: float32 [1536], replicated, may hold values from 0.5 to 1.5
- head_params: float32 [3, 24], replicated, as said below
Outputs:
- out: bfloat16 [16, 1024, 1024], P('fsdp', 'seq')
- d_tokens: float32 [16, 1024, 1024], P('fsdp', 'seq')
- g_w_in: float32 [1024, 4096], P('fsdp', 'seq')
- g_w_dt: float32 [1024, 24], P('fsdp')
- g_w_out: float32 [2048, 1024], P('fsdp', 'seq')
- g_w_gate_up: float32 [1024, 4096], P('fsdp', 'seq')
- g_w_down: float32 [2048, 1024], P('fsdp', 'seq')
- g_norm_gains: float32 [2, 1024], replicated
- g_conv_params: float32 [5, 1792], replicated
- g_ssm_gain: float32 [1536], replicated
- g_head_params: float32 [3, 24], replicated
The draws below stay inside these ranges and needn't reach their ends.
Inputs may be any that keep to these rules, and one draw needn't show every extreme that they name: `doc_start`: each row of 1024 positions holds documents laid end to end; a position's value is the first position of its document; the first document begins at 0; a middle document begins before position 512 and ends after position 512; in some row the last document is the final position alone. `head_params`: row 0 holds each head's log decay rate, row 1 its step-size bias, row 2 its skip coefficient.
All inputs are finite; a program needn't handle non-finite values.
Results may differ from the reference program's by a relative error of at most 0.017.
Values may be sent and summed in bfloat16 or wider, within the bound.
A program may use at most 256 MiB of HBM per device.

```python
import math
import jax
import jax.numpy as jnp
from jax import lax

D = 1024
FF = 2048
HEADS = 8
KV_HEADS = 2
HEAD_DIM = 64
SSM_HEADS = 24
SSM_DIM = 64
STATE = 128
CONV = 4
LENGTH = 1024
SPAN = 512
BATCH = 16
D_SSM = 1536
XBC = 1792
IN_W = 4096
MIX_W = 2048


def draw_doc_start(key, part):
    key = jax.random.fold_in(key, 11)
    first_key, last_key = jax.random.split(key)
    first = jax.random.randint(first_key, (BATCH, 1), 1, SPAN)
    final = jax.random.randint(last_key, (BATCH, 1), LENGTH - SPAN + 1, LENGTH)
    final = final.at[0, 0].set(LENGTH - 1)
    where_at = jnp.arange(LENGTH, dtype=jnp.int32)[None, :]
    return jnp.where(where_at < first, 0, jnp.where(where_at < final, first, final)).astype(jnp.int32)


def draw_head_params(key, part):
    key = jax.random.fold_in(key, 7)
    keys = jax.random.split(key, 5)
    base_step = jnp.exp(jax.random.uniform(keys[0], (SSM_HEADS,), jnp.float32, jnp.log(0.01), jnp.log(0.1)))
    bias = jnp.log(jnp.expm1(base_step))
    slow_share = 0.5
    slow = jax.random.uniform(keys[1], (SSM_HEADS,), jnp.float32) < slow_share
    reach = jnp.exp(jax.random.uniform(keys[2], (SSM_HEADS,), jnp.float32, jnp.log(0.3), 0.0))
    memory = LENGTH / jax.random.uniform(keys[3], (SSM_HEADS,), jnp.float32, 20.0, 34.0)
    rate = jnp.where(slow, reach / (1.65 * base_step * LENGTH), 1.0 / (1.65 * base_step * memory))
    skip = jax.random.uniform(keys[4], (SSM_HEADS,), jnp.float32, 0.5, 1.5)
    return jnp.stack([jnp.log(rate), bias, skip]).astype(jnp.float32)


def levels(rng, shape, pieces, low, high):
    level = 1.0
    for position, blocks in pieces:
        draws = jax.random.uniform(jax.random.fold_in(jax.random.fold_in(rng, 6), position), (blocks,), jnp.float32, low / len(pieces), high / len(pieces))
        level = level * jnp.repeat(jnp.exp(draws), shape[position] // blocks).reshape((-1,) + (1,) * (len(shape) - 1 - position))
    return level


def noise(stream_key, dims, deviation, limit, cuts=(), kind=jnp.bfloat16):
    loudness = levels(stream_key, dims, cuts, -0.22, 0.18) if cuts else 1.0
    entries = jax.random.normal(stream_key, dims, jnp.float32) * deviation * loudness
    return jnp.minimum(jnp.maximum(entries, -limit), limit).astype(kind)


def setup_inputs(seed: int = 0) -> dict:
    key_list = jax.random.split(jax.random.key(seed), 13)
    tokens = noise(key_list[0], (BATCH, LENGTH, D), 1.0, 6.0, ((0, 16), (1, 2)))
    cotangent = noise(key_list[1], (BATCH, LENGTH, D), 1.0, 6.0, ((0, 16), (1, 2)))
    doc_start = draw_doc_start(jax.random.fold_in(key_list[12], 71), 0)
    w_in = noise(key_list[3], (D, IN_W), D ** -0.5, 0.1875, ((0, 16), (1, 2)))
    w_dt = noise(key_list[4], (D, SSM_HEADS), D ** -0.5, 0.1875, ((0, 16),))
    w_out = noise(key_list[5], (MIX_W, D), D ** -0.5, 0.1875, ((0, 16), (1, 2)))
    w_gate_up = noise(key_list[6], (D, 2 * FF), D ** -0.5, 0.1875, ((0, 16), (1, 2)))
    w_down = noise(key_list[7], (FF, D), FF ** -0.5, 0.125, ((0, 16), (1, 2)))
    norm_gains = jnp.clip(1.0 + 0.1 * jax.random.normal(key_list[8], (2, D), jnp.float32), 0.5, 1.5)
    conv_params = jnp.clip(jax.random.uniform(key_list[9], (CONV + 1, XBC), jnp.float32, -0.5, 0.5), -0.5, 0.5)
    ssm_gain = jnp.clip(1.0 + 0.1 * jax.random.normal(key_list[10], (D_SSM,), jnp.float32), 0.5, 1.5)
    head_params = draw_head_params(jax.random.fold_in(key_list[12], 71), 0)
    return {"tokens": tokens, "cotangent": cotangent, "doc_start": doc_start, "w_in": w_in, "w_dt": w_dt, "w_out": w_out, "w_gate_up": w_gate_up, "w_down": w_down, "norm_gains": norm_gains, "conv_params": conv_params, "ssm_gain": ssm_gain, "head_params": head_params}


EPSILON = 1e-05
PRECISE = lax.Precision.HIGHEST

@jax.custom_vjp
def low(v):
    return lax.optimization_barrier(v.astype(jnp.bfloat16)).astype(jnp.float32)

@jax.custom_vjp
def low_back(v):
    return v

def low_keep(v):
    return (low(v), None)

def low_pass(kept, grad):
    return (grad,)

def back_keep(v):
    return (v, None)

def back_low(kept, grad):
    return (low(grad),)
low.defvjp(low_keep, low_pass)
low_back.defvjp(back_keep, back_low)

def rms_norm(values, gain):
    return values * lax.rsqrt(lax.optimization_barrier(jnp.mean(values * values, axis=-1, keepdims=True)) + EPSILON) * gain

def conv_pieces(extended, conv_params, dt_raw, head_params, valid):
    length = dt_raw.shape[1]
    summed = conv_params[CONV] + jnp.zeros((extended.shape[0], length, XBC), jnp.float32)
    for lagged in range(CONV):
        offset = CONV - 1 - lagged
        summed = summed + conv_params[lagged] * extended[:, offset:offset + length, :] * valid[lagged][..., None]
    activated = jax.nn.silu(summed)
    inputs = activated[..., :D_SSM].reshape(activated.shape[0], length, SSM_HEADS, SSM_DIM)
    b_proj = activated[..., D_SSM:D_SSM + STATE]
    c_proj = activated[..., D_SSM + STATE:]
    step_size = jax.nn.softplus(dt_raw + head_params[1])
    return (inputs, b_proj, c_proj, step_size, -jnp.exp(head_params[0]) * step_size)

def block_summary(inputs, b_proj, step_size, cumul, tail_mask, alive):
    final = cumul[:, -1, :]
    decay = jnp.exp(final) * alive[:, None]
    weights = jnp.exp(final[:, None, :] - cumul) * step_size * tail_mask[..., None]
    state = jnp.einsum('sph,sphd,spn->shdn', weights, inputs, b_proj, precision=PRECISE)
    return (decay, state)

def block_output(inputs, b_proj, c_proj, step_size, cumul, head_params, entering, gate_in, ssm_gain, inner_mask, carry_mask):
    gram = jnp.einsum('stn,srn->str', c_proj, b_proj, precision=PRECISE)
    spread = cumul[:, :, None, :] - cumul[:, None, :, :]
    decays = jnp.exp(jnp.where(inner_mask[..., None], spread, -1e+30))
    weights = decays * (gram[..., None] * step_size[:, None, :, :])
    within = jnp.einsum('strh,srhd->sthd', weights, inputs, precision=PRECISE)
    entry = jnp.exp(cumul) * carry_mask[..., None]
    incoming = jnp.einsum('sth,shdn,stn->sthd', entry, entering, c_proj, precision=PRECISE)
    output = within + incoming + head_params[2][:, None] * inputs
    output = output.reshape(output.shape[0], output.shape[1], D_SSM) * jax.nn.silu(gate_in)
    return rms_norm(output, ssm_gain)

def into_blocks(array, count):
    return array.reshape((count, 1, array.shape[1] // count) + array.shape[2:])

def layer(hidden, starts, w_in, w_dt, w_out, w_gate_up, w_down, norm_gains, conv_params, ssm_gain, head_params):
    share = HEADS // KV_HEADS
    q_width = HEADS * HEAD_DIM
    kv_width = KV_HEADS * HEAD_DIM
    base = q_width + 2 * kv_width
    where_at = jnp.arange(LENGTH, dtype=jnp.int32)
    normed = low(rms_norm(hidden, norm_gains[0]))
    projected = low_back(low(jnp.dot(normed, w_in, precision=PRECISE)))
    dt_raw = low_back(jnp.dot(normed, w_dt, precision=PRECISE))
    queries = projected[:, :q_width].reshape(LENGTH, KV_HEADS, share, HEAD_DIM)
    keys = projected[:, q_width:q_width + kv_width].reshape(LENGTH, KV_HEADS, HEAD_DIM)
    values = projected[:, q_width + kv_width:base].reshape(LENGTH, KV_HEADS, HEAD_DIM)
    gate_in = projected[:, base:base + D_SSM]
    conv_in = projected[:, base + D_SSM:]
    scores = low_back(jnp.einsum('tkgd,rkd->kgtr', queries, keys, precision=PRECISE) * HEAD_DIM ** (-0.5))
    allowed = (where_at[None, :] <= where_at[:, None]) & (where_at[None, :] >= starts[:, None])
    attn_probs = jax.nn.softmax(jnp.where(allowed, scores, -1e+30), axis=-1)
    attended = low_back(low(jnp.einsum('kgtr,rkd->tkgd', low(attn_probs), values, precision=PRECISE))).reshape(LENGTH, q_width)
    extended = jnp.concatenate([jnp.zeros((CONV - 1, XBC), jnp.float32), conv_in], axis=0)[None]
    valid = jnp.stack([where_at - lagged >= starts for lagged in range(CONV)]).astype(jnp.float32)[:, None]
    inputs, b_proj, c_proj, step_size, log_decay = conv_pieces(extended, conv_params, dt_raw[None], head_params, valid)
    block_rows = math.gcd(LENGTH, 128)
    count = LENGTH // block_rows
    items = (into_blocks(inputs, count), into_blocks(b_proj, count), into_blocks(c_proj, count), into_blocks(step_size, count), into_blocks(log_decay, count), into_blocks(gate_in[None], count), into_blocks(starts[None], count), into_blocks(where_at[None], count))

    def mamba_step(entering, item):
        x_blk, b_blk, c_blk, dt_blk, ld_blk, z_blk, st_blk, pos_blk = item
        block_start = pos_blk[0, 0]
        cumul = jnp.cumsum(ld_blk, axis=1)
        inner = (pos_blk[:, None, :] <= pos_blk[:, :, None]) & (pos_blk[:, None, :] >= st_blk[:, :, None])
        carry_mask = (st_blk < block_start).astype(jnp.float32)
        tail_mask = (pos_blk >= st_blk[:, -1:]).astype(jnp.float32)
        alive = (st_blk[:, -1] < block_start).astype(jnp.float32)
        output = block_output(x_blk, b_blk, c_blk, dt_blk, cumul, head_params, entering, z_blk, ssm_gain, inner, carry_mask)
        decay, state = block_summary(x_blk, b_blk, dt_blk, cumul, tail_mask, alive)
        return (decay[:, :, None, None] * entering + state, output)
    initial = jnp.zeros((1, SSM_HEADS, SSM_DIM, STATE), jnp.float32)
    _, mamba_out = lax.scan(jax.checkpoint(mamba_step), initial, items)
    mamba_out = low(mamba_out.reshape(LENGTH, D_SSM))
    mixed_in = jnp.concatenate([attended, mamba_out], axis=1)
    second = hidden + low_back(jnp.dot(mixed_in, w_out, precision=PRECISE))
    normed2 = low(rms_norm(second, norm_gains[1]))
    paired = low_back(jnp.dot(normed2, w_gate_up, precision=PRECISE))
    activ = low(jax.nn.silu(paired[:, :FF]) * paired[:, FF:])
    return second + jnp.dot(activ, w_down, precision=PRECISE)

def reference(tokens, cotangent, doc_start, w_in, w_dt, w_out, w_gate_up, w_down, norm_gains, conv_params, ssm_gain, head_params):

    def forward(tok_f, wi_f, wdt_f, wo_f, wgu_f, wdn_f, gains_f, conv_f, sgain_f, hp_f):

        def per_sequence(carry_zero, item):
            hidden, starts = item
            return (carry_zero, layer(hidden, starts, wi_f, wdt_f, wo_f, wgu_f, wdn_f, gains_f, conv_f, sgain_f, hp_f))
        _, outputs = lax.scan(jax.checkpoint(per_sequence), jnp.zeros((), jnp.float32), (tok_f, doc_start))
        return outputs
    result, pullback = jax.vjp(forward, tokens.astype(jnp.float32), w_in.astype(jnp.float32), w_dt.astype(jnp.float32), w_out.astype(jnp.float32), w_gate_up.astype(jnp.float32), w_down.astype(jnp.float32), norm_gains, conv_params, ssm_gain, head_params)
    grads = pullback(cotangent.astype(jnp.float32))
    return (result.astype(jnp.bfloat16), grads[0], grads[1], grads[2], grads[3], grads[4], grads[5], grads[6], grads[7], grads[8], grads[9])
```

```python
import math
from functools import partial

import jax
import jax.numpy as jnp
from jax import lax
from jax.sharding import PartitionSpec as P

FF = 2048
HEADS = 8
KV_HEADS = 2
HEAD_DIM = 64
SSM_HEADS = 24
SSM_DIM = 64
STATE = 128
CONV = 4
D_SSM = 1536
XBC = 1792


EPSILON = 1e-05
PRECISE = lax.Precision.HIGHEST


def passed_along(block, axis, distance):
    devices = range(lax.axis_size(axis))
    route = [(i - distance, i) for i in devices if i - distance in devices]
    return lax.ppermute(block, axis, route)


def entering_2(array, axis, combine, identity):
    devices, index = (lax.axis_size(axis), lax.axis_index(axis))
    everything = jax.tree.map(
        lambda part, kind: lax.all_gather(part.astype(kind), axis),
        array,
        (jnp.bfloat16, jnp.bfloat16),
    )
    start = jax.tree.map(
        lambda part, zero: jnp.broadcast_to(jnp.asarray(zero, part.dtype), part.shape),
        array,
        identity,
    )

    def lap(k, before):
        reached = k < index
        new = combine(
            before, jax.tree.map(lambda part, own: part[k].astype(own.dtype), everything, array)
        )
        return jax.tree.map(lambda a, b: jnp.where(reached, a, b), new, before)

    return lax.fori_loop(0, devices, lap, start)


def prefix_2(array, axis, join, neutral):
    count = lax.axis_size(axis)
    place = lax.axis_index(axis)
    ahead = count - 1 - place
    gathered = jax.tree.map(
        lambda a, kind: lax.all_gather(a.astype(kind), axis),
        array,
        jax.tree.map(lambda a: jnp.bfloat16 if a.dtype == jnp.float32 else a.dtype, array),
    )
    state = jax.tree.map(lambda a, e: jnp.zeros_like(a) + jnp.asarray(e, a.dtype), array, neutral)

    def one(lap, state):
        source = count - 1 - lap
        return join(
            state,
            jax.tree.map(
                lambda a, own: lax.dynamic_index_in_dim(a, source, 0, False).astype(own.dtype),
                gathered,
                array,
            ),
        )

    return lax.fori_loop(0, ahead, one, state)


def rms_norm(values, gain):
    return values * lax.rsqrt(jnp.mean(values * values, axis=-1, keepdims=True) + EPSILON) * gain


def swiglu(paired):
    return jax.nn.silu(paired[:, :FF]) * paired[:, FF:]


def times_rows(left, weight):
    return lax.dot_general(
        left, weight, (((1,), (1,)), ((), ())), preferred_element_type=jnp.float32
    )


def outer_total(left, right):
    return lax.dot_general(
        left, right, (((0,), (0,)), ((), ())), preferred_element_type=jnp.float32
    )


def seq_gather(blocks):
    count, place = lax.axis_size("seq"), lax.axis_index("seq")
    rows, cols = blocks.shape
    whole = jnp.zeros((rows, count * cols), blocks.dtype)
    whole = lax.dynamic_update_slice(whole, blocks, (0, place * cols))
    for hop in range(1, count):
        route = [(d, (d + hop) % count) for d in range(count)]
        came = lax.ppermute(blocks, "seq", route)
        source = lax.rem(place - hop + count, count)
        whole = lax.dynamic_update_slice(whole, came, (0, source * cols))
    return whole


def seq_scatter(pick):
    count, place = lax.axis_size("seq"), lax.axis_index("seq")
    total = pick(place).astype(jnp.float32)
    for hop in range(1, count):
        route = [(d, (d + hop) % count) for d in range(count)]
        target = lax.rem(place + hop, count)
        total = total + lax.ppermute(pick(target), "seq", route).astype(jnp.float32)
    return total


def columns(array, place, width):
    return lax.dynamic_slice_in_dim(array, place * width, width, 1)


def per_channel(array):
    return jnp.repeat(array, SSM_DIM, axis=-1)


def conv_pieces(extended, conv_params, dt_raw, head_params, valid, chunk):
    num, length = dt_raw.shape[:2]
    summed = conv_params[CONV] + jnp.zeros((num, length, XBC), jnp.float32)
    for lagged in range(CONV):
        offset = CONV - 1 - lagged
        summed = (
            summed
            + conv_params[lagged]
            * extended[:, offset : offset + length, :]
            * valid[lagged][..., None]
        )
    activated = jax.nn.silu(summed).reshape(num, length // chunk, chunk, XBC)
    inputs = activated[..., :D_SSM]
    b_proj = activated[..., D_SSM : D_SSM + STATE]
    c_proj = activated[..., D_SSM + STATE :]
    step_size = jax.nn.softplus(dt_raw + head_params[1])
    step_size = step_size.reshape(num, length // chunk, chunk, SSM_HEADS)
    lower = jnp.tril(jnp.ones((chunk, chunk), jnp.float32))
    cumul = jnp.einsum(
        "tr,scrh->scth", lower, -jnp.exp(head_params[0]) * step_size, precision=PRECISE
    )
    return (inputs, b_proj, c_proj, step_size, cumul)


def block_summary(inputs, b_proj, step_size, cumul, tail_mask, alive):
    final = cumul[:, :, -1, :]
    decay = jnp.exp(final) * alive[..., None]
    weights = jnp.exp(final[:, :, None, :] - cumul) * step_size * tail_mask[..., None]
    state = jnp.einsum(
        "scpe,scpn->scen", per_channel(weights) * inputs, b_proj, preferred_element_type=jnp.float32
    )
    num, chunks = state.shape[:2]
    state = state.reshape(num, chunks, SSM_HEADS, SSM_DIM, STATE)
    reach = jnp.ones_like(decay[:, 0])
    carried = jnp.zeros_like(state[:, 0])
    reaches, carries = [], []
    for k in range(chunks):
        reaches.append(reach)
        carries.append(carried)
        carried = decay[:, k][:, :, None, None] * carried + state[:, k]
        reach = reach * decay[:, k]
    return (reach, carried, jnp.stack(reaches, 1), jnp.stack(carries, 1))


def block_output(
    inputs,
    b_proj,
    c_proj,
    step_size,
    cumul,
    head_params,
    reaches,
    carries,
    entering,
    gate_in,
    ssm_gain,
    inner_mask,
    carry_mask,
):
    num, chunks, chunk = inputs.shape[:3]
    gram = jnp.einsum("sctn,scrn->sctr", c_proj, b_proj, preferred_element_type=jnp.float32)
    cumul_h = jnp.swapaxes(cumul, 2, 3)
    step_h = jnp.swapaxes(step_size, 2, 3)
    spread = cumul_h[..., :, None] - cumul_h[..., None, :]
    decays = jnp.exp(jnp.where(inner_mask[:, :, None], spread, -1e30))
    weights = decays * (gram[:, :, None] * step_h[..., None, :])
    heads = inputs.reshape(num, chunks, chunk, SSM_HEADS, SSM_DIM)
    within = jnp.einsum(
        "schtr,scrhd->scthd", weights, heads, preferred_element_type=jnp.float32
    ).reshape(inputs.shape)
    entry = jnp.exp(cumul) * carry_mask[..., None]
    states = carries + reaches[..., None, None] * entering[:, None]
    states = states.reshape(num, chunks, D_SSM, STATE)
    incoming = per_channel(entry) * jnp.einsum(
        "scen,sctn->scte", states, c_proj, preferred_element_type=jnp.float32
    )
    output = within + incoming + per_channel(head_params[2]) * inputs
    output = output.reshape(num, chunks * chunk, D_SSM) * jax.nn.silu(gate_in)
    return rms_norm(output, ssm_gain)


def join_states(earlier, later):
    return (earlier[0] * later[0], later[0][:, :, None, None] * earlier[1] + later[1])


def join_grads(earlier, later):
    return (later[0] * earlier[0], later[1] + later[0][:, :, None, None] * earlier[1])


def body(
    tokens,
    cotangent,
    doc_start,
    w_in,
    w_dt,
    w_out,
    w_gate_up,
    w_down,
    norm_gains,
    conv_params,
    ssm_gain,
    head_params,
):
    num_seqs, span_len, model_width = tokens.shape
    num_rows = num_seqs * span_len
    block_start = lax.axis_index("seq") * span_len
    q_width = HEADS * HEAD_DIM
    kv_width = KV_HEADS * HEAD_DIM
    head_share = HEADS // KV_HEADS
    att_scale = HEAD_DIM ** (-0.5)
    rim_len = CONV - 1
    chunk = math.gcd(span_len, 128)
    chunks = span_len // chunk
    base_col = q_width + 2 * kv_width
    cols_in, cols_out, cols_gu, cols_down = (
        seq_gather(w_in),
        seq_gather(w_out),
        seq_gather(w_gate_up),
        seq_gather(w_down),
    )
    full_in, full_dt, full_out, full_gu, full_down = (
        lax.all_gather(cols_in, "fsdp", axis=0, tiled=True),
        lax.all_gather(w_dt, "fsdp", axis=0, tiled=True),
        lax.all_gather(cols_out, "fsdp", axis=0, tiled=True),
        lax.all_gather(cols_gu, "fsdp", axis=0, tiled=True),
        lax.all_gather(cols_down, "fsdp", axis=0, tiled=True),
    )
    hidden = tokens.reshape(num_rows, model_width).astype(jnp.float32)
    normed_f, norm1_back = jax.vjp(rms_norm, hidden, norm_gains[0])
    normed = normed_f.astype(jnp.bfloat16)
    projected = jnp.dot(normed, full_in, preferred_element_type=jnp.float32).astype(jnp.bfloat16)
    dt_raw = jnp.dot(normed, full_dt, preferred_element_type=jnp.float32)
    queries = projected[:, :q_width].reshape(num_rows, KV_HEADS, head_share, HEAD_DIM)
    kv_all = lax.all_gather(projected[:, q_width:base_col], "seq", axis=0, tiled=True)
    total_keys = kv_all.shape[0]
    keys_all = kv_all[:, :kv_width].reshape(total_keys, KV_HEADS, HEAD_DIM)
    values_all = kv_all[:, kv_width:].reshape(total_keys, KV_HEADS, HEAD_DIM)
    row_index = jnp.arange(num_rows, dtype=jnp.int32)
    q_seq = row_index // span_len
    q_pos = block_start + row_index % span_len
    row_starts = doc_start.reshape(num_rows)
    key_index = jnp.arange(total_keys, dtype=jnp.int32)
    key_within = key_index % num_rows
    k_seq = key_within // span_len
    k_pos = key_index // num_rows * span_len + key_within % span_len
    allowed = (
        (k_seq[None, :] == q_seq[:, None])
        & (k_pos[None, :] <= q_pos[:, None])
        & (k_pos[None, :] >= row_starts[:, None])
    )
    scores = (
        jnp.einsum("tkgd,ckd->kgtc", queries, keys_all, preferred_element_type=jnp.float32)
        * att_scale
    )
    scores = jnp.where(allowed, scores, -1e30)
    row_max = jnp.max(scores, axis=-1, keepdims=True)
    shifted = jnp.exp(scores - row_max)
    attn_probs = shifted / jnp.sum(shifted, axis=-1, keepdims=True)
    probs_low = attn_probs.astype(jnp.bfloat16)
    attended = (
        jnp.einsum("kgtc,ckd->tkgd", probs_low, values_all, preferred_element_type=jnp.float32)
        .reshape(num_rows, q_width)
        .astype(jnp.bfloat16)
    )
    gate_in = (
        projected[:, base_col : base_col + D_SSM]
        .astype(jnp.float32)
        .reshape(num_seqs, span_len, D_SSM)
    )
    conv_in = projected[:, base_col + D_SSM :].reshape(num_seqs, span_len, XBC)
    before = passed_along(conv_in[:, span_len - rim_len :, :], "seq", 1)
    extended = jnp.concatenate([before, conv_in], axis=1).astype(jnp.float32)
    positions = block_start + jnp.arange(span_len, dtype=jnp.int32)
    valid = jnp.stack([positions[None, :] - lagged >= doc_start for lagged in range(CONV)]).astype(
        jnp.float32
    )
    pieces, pieces_back = jax.vjp(
        partial(conv_pieces, valid=valid, chunk=chunk),
        extended,
        conv_params,
        dt_raw.reshape(num_seqs, span_len, SSM_HEADS),
        head_params,
    )
    inputs, b_proj, c_proj, step_size, cumul = pieces
    starts = doc_start.reshape(num_seqs, chunks, chunk)
    places = positions.reshape(chunks, chunk)
    chunk_start = places[:, :1]
    tail_mask = (places >= starts[..., -1:]).astype(jnp.float32)
    alive_mask = (starts[..., -1] < places[:, 0]).astype(jnp.float32)
    summary, summary_back = jax.vjp(
        partial(block_summary, tail_mask=tail_mask, alive=alive_mask),
        inputs,
        b_proj,
        step_size,
        cumul,
    )
    unit_decay = jnp.ones_like(summary[0])
    empty_state = jnp.zeros_like(summary[1])
    prefix = entering_2((summary[0], summary[1]), "seq", join_states, (unit_decay, empty_state))
    entering = prefix[1]
    inner_mask = (places[:, None, :] <= places[:, :, None]) & (
        places[:, None, :] >= starts[..., None]
    )
    carry_mask = (starts < chunk_start).astype(jnp.float32)
    mamba_f, output_back = jax.vjp(
        partial(block_output, inner_mask=inner_mask, carry_mask=carry_mask),
        inputs,
        b_proj,
        c_proj,
        step_size,
        cumul,
        head_params,
        summary[2],
        summary[3],
        entering,
        gate_in,
        ssm_gain,
    )
    mamba_low = mamba_f.reshape(num_rows, D_SSM).astype(jnp.bfloat16)
    mixed_in = jnp.concatenate([attended, mamba_low], axis=1)
    second = hidden + jnp.dot(mixed_in, full_out, preferred_element_type=jnp.float32)
    normed2_f, norm2_back = jax.vjp(rms_norm, second, norm_gains[1])
    normed2 = normed2_f.astype(jnp.bfloat16)
    paired = jnp.dot(normed2, full_gu, preferred_element_type=jnp.float32)
    activ_f, activ_back = jax.vjp(swiglu, paired)
    activ = activ_f.astype(jnp.bfloat16)
    result = second + jnp.dot(activ, full_down, preferred_element_type=jnp.float32)
    upstream = cotangent.reshape(num_rows, model_width)
    grad_down = outer_total(activ, upstream)
    d_activ = times_rows(upstream, full_down)
    d_paired = activ_back(d_activ)[0].astype(jnp.bfloat16)
    grad_gu = outer_total(normed2, d_paired)
    grad_gu = grad_gu.astype(jnp.bfloat16)
    grad_gu, grad_down, d_paired = lax.optimization_barrier((grad_gu, grad_down.astype(jnp.bfloat16), d_paired))
    share_gu = lax.psum_scatter(grad_gu, "fsdp", scatter_dimension=0, tiled=True)
    d_normed2 = times_rows(d_paired, full_gu)
    d_second, d_gain2 = norm2_back(d_normed2)
    d_second = d_second + upstream.astype(jnp.float32)
    d_mixed = d_second.astype(jnp.bfloat16)
    grad_out = outer_total(mixed_in, d_mixed)
    grad_pair = jnp.concatenate([grad_down, grad_out.astype(jnp.bfloat16)], axis=1)
    grad_pair, d_mixed = lax.optimization_barrier((grad_pair, d_mixed))
    share_pair = lax.psum_scatter(grad_pair, "fsdp", scatter_dimension=0, tiled=True)
    d_mixed_in = times_rows(d_mixed, full_out)
    d_attended = (
        d_mixed_in[:, :q_width]
        .astype(jnp.bfloat16)
        .reshape(num_rows, KV_HEADS, head_share, HEAD_DIM)
    )
    d_mamba = d_mixed_in[:, q_width:].reshape(num_seqs, span_len, D_SSM)
    d_probs = jnp.einsum(
        "tkgd,ckd->kgtc", d_attended, values_all, preferred_element_type=jnp.float32
    )
    centre = jnp.sum(attn_probs * d_probs, axis=-1, keepdims=True)
    d_scores = (attn_probs * (d_probs - centre)).astype(jnp.bfloat16)
    d_queries = (
        jnp.einsum("kgtc,ckd->tkgd", d_scores, keys_all, preferred_element_type=jnp.float32)
        * att_scale
    ).reshape(num_rows, q_width)
    d_keys = (
        jnp.einsum("kgtc,tkgd->ckd", d_scores, queries, preferred_element_type=jnp.float32)
        * att_scale
    )
    d_values = jnp.einsum(
        "kgtc,tkgd->ckd", probs_low, d_attended, preferred_element_type=jnp.float32
    )
    d_kv = lax.psum_scatter(
        jnp.concatenate(
            [
                d_keys.reshape(num_rows * lax.axis_size("seq"), kv_width),
                d_values.reshape(num_rows * lax.axis_size("seq"), kv_width),
            ],
            axis=1,
        ).astype(jnp.bfloat16),
        "seq",
        scatter_dimension=0,
        tiled=True,
    ).astype(jnp.float32)
    g_inputs, g_bproj, g_cproj, g_step, g_cumul, g_head_out, g_reaches, g_carries, *g_rest = (
        output_back(d_mamba)
    )
    g_entering, g_gate, g_ssm = g_rest
    ahead = prefix_2((summary[0], g_entering), "seq", join_grads, (unit_decay, empty_state))
    state_grad = ahead[1]
    d_decay = jnp.sum(state_grad * entering, axis=(2, 3))
    s_inputs, s_bproj, s_step, s_cumul = summary_back(
        (d_decay, state_grad, g_reaches, g_carries)
    )
    d_extended, g_conv, d_dt_raw, g_head_in = pieces_back(
        (g_inputs + s_inputs, g_bproj + s_bproj, g_cproj, g_step + s_step, g_cumul + s_cumul)
    )
    from_next = passed_along(d_extended[:, :rim_len, :], "seq", -1)
    d_conv_in = d_extended[:, rim_len:, :] + jnp.pad(
        from_next, ((0, 0), (span_len - rim_len, 0), (0, 0))
    )
    d_projected = jnp.concatenate(
        [d_queries, d_kv, g_gate.reshape(num_rows, D_SSM), d_conv_in.reshape(num_rows, XBC)], axis=1
    ).astype(jnp.bfloat16)
    d_dt_low = d_dt_raw.reshape(num_rows, SSM_HEADS).astype(jnp.bfloat16)
    pad = jnp.zeros((num_rows, 128 - SSM_HEADS), jnp.bfloat16)
    grad_in = outer_total(normed, jnp.concatenate([d_projected, d_dt_low, pad], axis=1))
    share_in = lax.psum_scatter(
        grad_in.astype(jnp.bfloat16), "fsdp", scatter_dimension=0, tiled=True
    )
    d_normed = times_rows(d_projected, full_in) + times_rows(d_dt_low, full_dt)
    d_hidden, d_gain1 = norm1_back(d_normed)
    d_hidden = d_hidden + d_second
    width = model_width // lax.axis_size("seq")
    in_width = share_gu.shape[1] // lax.axis_size("seq")
    total_gu = seq_scatter(lambda k: columns(share_gu, k, in_width))
    total_pair = seq_scatter(
        lambda k: jnp.concatenate(
            [
                columns(share_pair[:, :model_width], k, width),
                columns(share_pair[:, model_width:], k, width),
            ],
            axis=1,
        )
    )
    in_cols = d_projected.shape[1]
    total_in = seq_scatter(
        lambda k: jnp.concatenate(
            [columns(share_in[:, :in_cols], k, in_width), share_in[:, in_cols:]], axis=1
        )
    )
    summed_small = lax.psum(
        (jnp.stack([d_gain1, d_gain2]), g_conv, g_ssm, g_head_out + g_head_in),
        ("fsdp", "seq"),
    )
    return (
        result.reshape(num_seqs, span_len, model_width).astype(jnp.bfloat16),
        d_hidden.reshape(num_seqs, span_len, model_width),
        total_in[:, :in_width],
        total_in[:, in_width : in_width + SSM_HEADS],
        total_pair[:, width:],
        total_gu,
        total_pair[:, :width],
        summed_small[0],
        summed_small[1],
        summed_small[2],
        summed_small[3],
    )


def solution(mesh):
    placed = (
        P("fsdp", "seq", None),
        P("fsdp", "seq", None),
        P("fsdp", "seq"),
        P("fsdp", "seq"),
        P("fsdp", None),
        P("fsdp", "seq"),
        P("fsdp", "seq"),
        P("fsdp", "seq"),
        P(),
        P(),
        P(),
        P(),
    )
    return jax.shard_map(
        body,
        mesh=mesh,
        in_specs=placed,
        out_specs=(
            P("fsdp", "seq", None),
            P("fsdp", "seq", None),
            P("fsdp", "seq"),
            P("fsdp", None),
            P("fsdp", "seq"),
            P("fsdp", "seq"),
            P("fsdp", "seq"),
            P(),
            P(),
            P(),
            P(),
        ),
        check_vma=False,
    )
```

```python
import math
from functools import partial

import jax
import jax.numpy as jnp
from jax import lax
from jax.sharding import PartitionSpec as P

FF = 2048
HEADS = 8
KV_HEADS = 2
HEAD_DIM = 64
SSM_HEADS = 24
SSM_DIM = 64
STATE = 128
CONV = 4
D_SSM = 1536
XBC = 1792


EPSILON = 1e-05
PRECISE = lax.Precision.HIGHEST


def passed_along(block, axis, distance):
    devices = range(lax.axis_size(axis))
    route = [(i - distance, i) for i in devices if i - distance in devices]
    return lax.ppermute(block, axis, route)


def entering_states(decay, state, direction):
    count = lax.axis_size("seq")
    rank = lax.axis_index("seq")
    if direction < 0:
        rank = count - 1 - rank
    decay = jnp.where(rank == 0, 1.0, passed_along(decay, "seq", direction))
    state = passed_along(state.astype(jnp.bfloat16), "seq", direction).astype(jnp.float32)
    reach = 1
    while reach < count - 1:
        earlier = passed_along(decay, "seq", direction * reach)
        lower = passed_along(state.astype(jnp.bfloat16), "seq", direction * reach)
        joined = decay[:, :, None, None] * lower.astype(jnp.float32) + state
        state = jnp.where(rank >= reach, joined, state)
        decay = jnp.where(rank >= reach, decay * earlier, decay)
        reach *= 2
    return state


def other_core(block):
    route = [(d, d + 1 - 2 * (d % 2)) for d in range(lax.axis_size("fsdp"))]
    return lax.ppermute(block, "fsdp", route)


def same_core():
    count = lax.axis_size("fsdp")
    return [list(range(0, count, 2)), list(range(1, count, 2))]


def chip_gather(block):
    rows, cols = block.shape
    chips = lax.axis_size("fsdp") // 2
    own = lax.all_gather(block, "fsdp", axis=0, tiled=True, axis_index_groups=same_core())
    other = other_core(own)
    first = lax.axis_index("fsdp") % 2 == 0
    even = jnp.where(first, own, other).reshape(chips, 1, rows, cols)
    odd = jnp.where(first, other, own).reshape(chips, 1, rows, cols)
    return jnp.concatenate([even, odd], axis=1).reshape(2 * chips * rows, cols)


def core_sums(grad):
    chips = lax.axis_size("fsdp") // 2
    rows = grad.shape[0] // (2 * chips)
    split = grad.reshape(chips, 2, rows, grad.shape[1])
    core = lax.axis_index("fsdp") % 2
    mine = lax.dynamic_index_in_dim(split, core, 1, False)
    came = other_core(lax.dynamic_index_in_dim(split, 1 - core, 1, False))
    return (mine.astype(jnp.float32) + came.astype(jnp.float32)).astype(jnp.bfloat16)


def chip_scatter(sums):
    chips, rows, cols = sums.shape
    return lax.psum_scatter(
        sums.reshape(chips * rows, cols),
        "fsdp",
        scatter_dimension=0,
        axis_index_groups=same_core(),
        tiled=True,
    )


def rms_norm(values, gain):
    return values * lax.rsqrt(jnp.mean(values * values, axis=-1, keepdims=True) + EPSILON) * gain


def swiglu(paired):
    return jax.nn.silu(paired[:, :FF]) * paired[:, FF:]


def times_rows(left, weight):
    return lax.dot_general(
        left, weight, (((1,), (1,)), ((), ())), preferred_element_type=jnp.float32
    )


def outer_total(left, right):
    return lax.dot_general(
        left, right, (((0,), (0,)), ((), ())), preferred_element_type=jnp.float32
    )


def seq_gather(block, axis):
    count, place = lax.axis_size("seq"), lax.axis_index("seq")
    size = block.shape[axis]
    shape = list(block.shape)
    shape[axis] *= count
    whole = jnp.zeros(shape, block.dtype)
    whole = lax.dynamic_update_slice_in_dim(whole, block, place * size, axis)
    for hop in range(1, count):
        route = [(d, (d + hop) % count) for d in range(count)]
        came = lax.ppermute(block, "seq", route)
        source = lax.rem(place - hop + count, count)
        whole = lax.dynamic_update_slice_in_dim(whole, came, source * size, axis)
    return whole


def seq_scatter(pick):
    count, place = lax.axis_size("seq"), lax.axis_index("seq")
    total = pick(place).astype(jnp.float32)
    for hop in range(1, count):
        route = [(d, (d + hop) % count) for d in range(count)]
        target = lax.rem(place + hop, count)
        total = total + lax.ppermute(pick(target), "seq", route).astype(jnp.float32)
    return total


def columns(array, place, width):
    return lax.dynamic_slice_in_dim(array, place * width, width, 1)


def per_channel(array):
    return jnp.repeat(array, SSM_DIM, axis=-1)


def conv_pieces(extended, conv_params, dt_raw, head_params, valid, chunk):
    num, length = dt_raw.shape[:2]
    summed = conv_params[CONV] + jnp.zeros((num, length, XBC), jnp.float32)
    for lagged in range(CONV):
        offset = CONV - 1 - lagged
        summed = (
            summed
            + conv_params[lagged]
            * extended[:, offset : offset + length, :]
            * valid[lagged][..., None]
        )
    activated = jax.nn.silu(summed).reshape(num, length // chunk, chunk, XBC)
    inputs = activated[..., :D_SSM]
    b_proj = activated[..., D_SSM : D_SSM + STATE]
    c_proj = activated[..., D_SSM + STATE :]
    step_size = jax.nn.softplus(dt_raw + head_params[1])
    step_size = step_size.reshape(num, length // chunk, chunk, SSM_HEADS)
    lower = jnp.tril(jnp.ones((chunk, chunk), jnp.float32))
    cumul = jnp.einsum(
        "tr,scrh->scth", lower, -jnp.exp(head_params[0]) * step_size, precision=PRECISE
    )
    return (inputs, b_proj, c_proj, step_size, cumul)


def block_summary(inputs, b_proj, step_size, cumul, tail_mask, alive):
    final = cumul[:, :, -1, :]
    decay = jnp.exp(final) * alive[..., None]
    weights = jnp.exp(final[:, :, None, :] - cumul) * step_size * tail_mask[..., None]
    state = jnp.einsum(
        "scpe,scpn->scen", per_channel(weights) * inputs, b_proj, preferred_element_type=jnp.float32
    )
    num, chunks = state.shape[:2]
    state = state.reshape(num, chunks, SSM_HEADS, SSM_DIM, STATE)
    reach = jnp.ones_like(decay[:, 0])
    carried = jnp.zeros_like(state[:, 0])
    reaches, carries = [], []
    for k in range(chunks):
        reaches.append(reach)
        carries.append(carried)
        carried = decay[:, k][:, :, None, None] * carried + state[:, k]
        reach = reach * decay[:, k]
    return (reach, carried, jnp.stack(reaches, 1), jnp.stack(carries, 1))


def block_output(
    inputs,
    b_proj,
    c_proj,
    step_size,
    cumul,
    head_params,
    reaches,
    carries,
    entering,
    gate_in,
    ssm_gain,
    inner_mask,
    carry_mask,
):
    num, chunks, chunk = inputs.shape[:3]
    gram = jnp.einsum("sctn,scrn->sctr", c_proj, b_proj, preferred_element_type=jnp.float32)
    cumul_h = jnp.swapaxes(cumul, 2, 3)
    step_h = jnp.swapaxes(step_size, 2, 3)
    spread = cumul_h[..., :, None] - cumul_h[..., None, :]
    decays = jnp.exp(jnp.where(inner_mask[:, :, None], spread, -1e30))
    weights = decays * (gram[:, :, None] * step_h[..., None, :])
    heads = inputs.reshape(num, chunks, chunk, SSM_HEADS, SSM_DIM)
    within = jnp.einsum(
        "schtr,scrhd->scthd", weights, heads, preferred_element_type=jnp.float32
    ).reshape(inputs.shape)
    entry = jnp.exp(cumul) * carry_mask[..., None]
    states = carries + reaches[..., None, None] * entering[:, None]
    states = states.reshape(num, chunks, D_SSM, STATE)
    incoming = per_channel(entry) * jnp.einsum(
        "scen,sctn->scte", states, c_proj, preferred_element_type=jnp.float32
    )
    output = within + incoming + per_channel(head_params[2]) * inputs
    output = output.reshape(num, chunks * chunk, D_SSM) * jax.nn.silu(gate_in)
    return rms_norm(output, ssm_gain)


def body(
    tokens,
    cotangent,
    doc_start,
    w_in,
    w_dt,
    w_out,
    w_gate_up,
    w_down,
    norm_gains,
    conv_params,
    ssm_gain,
    head_params,
):
    num_seqs, span_len, model_width = tokens.shape
    num_rows = num_seqs * span_len
    block_start = lax.axis_index("seq") * span_len
    q_width = HEADS * HEAD_DIM
    kv_width = KV_HEADS * HEAD_DIM
    head_share = HEADS // KV_HEADS
    att_scale = HEAD_DIM ** (-0.5)
    rim_len = CONV - 1
    chunk = math.gcd(span_len, 128)
    chunks = span_len // chunk
    base_col = q_width + 2 * kv_width
    cols_in, cols_out, cols_gu, cols_down = (
        seq_gather(w_in, 1),
        seq_gather(w_out, 1),
        seq_gather(w_gate_up, 1),
        seq_gather(w_down, 1),
    )
    full_in, full_dt, full_out, full_gu, full_down = (
        chip_gather(cols_in),
        lax.all_gather(w_dt, "fsdp", axis=0, tiled=True),
        chip_gather(cols_out),
        chip_gather(cols_gu),
        chip_gather(cols_down),
    )
    hidden = tokens.reshape(num_rows, model_width).astype(jnp.float32)
    normed_f, norm1_back = jax.vjp(rms_norm, hidden, norm_gains[0])
    normed = normed_f.astype(jnp.bfloat16)
    projected = jnp.dot(normed, full_in, preferred_element_type=jnp.float32).astype(jnp.bfloat16)
    dt_raw = jnp.dot(normed, full_dt, preferred_element_type=jnp.float32)
    queries = projected[:, :q_width].reshape(num_rows, KV_HEADS, head_share, HEAD_DIM)
    kv_all = seq_gather(projected[:, q_width:base_col], 0)
    total_keys = kv_all.shape[0]
    keys_all = kv_all[:, :kv_width].reshape(total_keys, KV_HEADS, HEAD_DIM)
    values_all = kv_all[:, kv_width:].reshape(total_keys, KV_HEADS, HEAD_DIM)
    row_index = jnp.arange(num_rows, dtype=jnp.int32)
    q_seq = row_index // span_len
    q_pos = block_start + row_index % span_len
    row_starts = doc_start.reshape(num_rows)
    key_index = jnp.arange(total_keys, dtype=jnp.int32)
    key_within = key_index % num_rows
    k_seq = key_within // span_len
    k_pos = key_index // num_rows * span_len + key_within % span_len
    allowed = (
        (k_seq[None, :] == q_seq[:, None])
        & (k_pos[None, :] <= q_pos[:, None])
        & (k_pos[None, :] >= row_starts[:, None])
    )
    scores = (
        jnp.einsum("tkgd,ckd->kgtc", queries, keys_all, preferred_element_type=jnp.float32)
        * att_scale
    )
    scores = jnp.where(allowed, scores, -1e30)
    row_max = jnp.max(scores, axis=-1, keepdims=True)
    shifted = jnp.exp(scores - row_max)
    attn_probs = shifted / jnp.sum(shifted, axis=-1, keepdims=True)
    probs_low = attn_probs.astype(jnp.bfloat16)
    attended = (
        jnp.einsum("kgtc,ckd->tkgd", probs_low, values_all, preferred_element_type=jnp.float32)
        .reshape(num_rows, q_width)
        .astype(jnp.bfloat16)
    )
    gate_in = (
        projected[:, base_col : base_col + D_SSM]
        .astype(jnp.float32)
        .reshape(num_seqs, span_len, D_SSM)
    )
    conv_in = projected[:, base_col + D_SSM :].reshape(num_seqs, span_len, XBC)
    before = passed_along(conv_in[:, span_len - rim_len :, :], "seq", 1)
    extended = jnp.concatenate([before, conv_in], axis=1).astype(jnp.float32)
    positions = block_start + jnp.arange(span_len, dtype=jnp.int32)
    valid = jnp.stack([positions[None, :] - lagged >= doc_start for lagged in range(CONV)]).astype(
        jnp.float32
    )
    pieces, pieces_back = jax.vjp(
        partial(conv_pieces, valid=valid, chunk=chunk),
        extended,
        conv_params,
        dt_raw.reshape(num_seqs, span_len, SSM_HEADS),
        head_params,
    )
    inputs, b_proj, c_proj, step_size, cumul = pieces
    starts = doc_start.reshape(num_seqs, chunks, chunk)
    places = positions.reshape(chunks, chunk)
    chunk_start = places[:, :1]
    tail_mask = (places >= starts[..., -1:]).astype(jnp.float32)
    alive_mask = (starts[..., -1] < places[:, 0]).astype(jnp.float32)
    summary, summary_back = jax.vjp(
        partial(block_summary, tail_mask=tail_mask, alive=alive_mask),
        inputs,
        b_proj,
        step_size,
        cumul,
    )
    entering = entering_states(summary[0], summary[1], 1)
    inner_mask = (places[:, None, :] <= places[:, :, None]) & (
        places[:, None, :] >= starts[..., None]
    )
    carry_mask = (starts < chunk_start).astype(jnp.float32)
    mamba_f, output_back = jax.vjp(
        partial(block_output, inner_mask=inner_mask, carry_mask=carry_mask),
        inputs,
        b_proj,
        c_proj,
        step_size,
        cumul,
        head_params,
        summary[2],
        summary[3],
        entering,
        gate_in,
        ssm_gain,
    )
    mamba_low = mamba_f.reshape(num_rows, D_SSM).astype(jnp.bfloat16)
    mixed_in = jnp.concatenate([attended, mamba_low], axis=1)
    second = hidden + jnp.dot(mixed_in, full_out, preferred_element_type=jnp.float32)
    normed2_f, norm2_back = jax.vjp(rms_norm, second, norm_gains[1])
    normed2 = normed2_f.astype(jnp.bfloat16)
    paired = jnp.dot(normed2, full_gu, preferred_element_type=jnp.float32)
    activ_f, activ_back = jax.vjp(swiglu, paired)
    activ = activ_f.astype(jnp.bfloat16)
    result = second + jnp.dot(activ, full_down, preferred_element_type=jnp.float32)
    upstream = cotangent.reshape(num_rows, model_width)
    grad_down = outer_total(activ, upstream)
    d_activ = times_rows(upstream, full_down)
    d_paired = activ_back(d_activ)[0].astype(jnp.bfloat16)
    grad_gu = outer_total(normed2, d_paired)
    grad_gu, grad_down, d_paired = lax.optimization_barrier(
        (grad_gu.astype(jnp.bfloat16), grad_down.astype(jnp.bfloat16), d_paired)
    )
    share_gu = chip_scatter(core_sums(grad_gu))
    d_normed2 = times_rows(d_paired, full_gu)
    d_second, d_gain2 = norm2_back(d_normed2)
    d_second = d_second + upstream.astype(jnp.float32)
    d_mixed = d_second.astype(jnp.bfloat16)
    grad_out = outer_total(mixed_in, d_mixed)
    grad_out, d_mixed = lax.optimization_barrier((grad_out.astype(jnp.bfloat16), d_mixed))
    share_pair = chip_scatter(
        jnp.concatenate([core_sums(grad_down), core_sums(grad_out)], axis=1)
    )
    d_mixed_in = times_rows(d_mixed, full_out)
    d_attended = (
        d_mixed_in[:, :q_width]
        .astype(jnp.bfloat16)
        .reshape(num_rows, KV_HEADS, head_share, HEAD_DIM)
    )
    d_mamba = d_mixed_in[:, q_width:].reshape(num_seqs, span_len, D_SSM)
    d_probs = jnp.einsum(
        "tkgd,ckd->kgtc", d_attended, values_all, preferred_element_type=jnp.float32
    )
    centre = jnp.sum(attn_probs * d_probs, axis=-1, keepdims=True)
    d_scores = (attn_probs * (d_probs - centre)).astype(jnp.bfloat16)
    d_queries = (
        jnp.einsum("kgtc,ckd->tkgd", d_scores, keys_all, preferred_element_type=jnp.float32)
        * att_scale
    ).reshape(num_rows, q_width)
    d_keys = (
        jnp.einsum("kgtc,tkgd->ckd", d_scores, queries, preferred_element_type=jnp.float32)
        * att_scale
    )
    d_values = jnp.einsum(
        "kgtc,tkgd->ckd", probs_low, d_attended, preferred_element_type=jnp.float32
    )
    d_kv_all = jnp.concatenate(
        [d_keys.reshape(total_keys, kv_width), d_values.reshape(total_keys, kv_width)], axis=1
    ).astype(jnp.bfloat16)
    d_kv = seq_scatter(lambda k: lax.dynamic_slice_in_dim(d_kv_all, k * num_rows, num_rows, 0))
    g_inputs, g_bproj, g_cproj, g_step, g_cumul, g_head_out, g_reaches, g_carries, *g_rest = (
        output_back(d_mamba)
    )
    g_entering, g_gate, g_ssm = g_rest
    state_grad = entering_states(summary[0], g_entering, -1)
    d_decay = jnp.sum(state_grad * entering, axis=(2, 3))
    s_inputs, s_bproj, s_step, s_cumul = summary_back(
        (d_decay, state_grad, g_reaches, g_carries)
    )
    d_extended, g_conv, d_dt_raw, g_head_in = pieces_back(
        (g_inputs + s_inputs, g_bproj + s_bproj, g_cproj, g_step + s_step, g_cumul + s_cumul)
    )
    from_next = passed_along(d_extended[:, :rim_len, :], "seq", -1)
    d_conv_in = d_extended[:, rim_len:, :] + jnp.pad(
        from_next, ((0, 0), (span_len - rim_len, 0), (0, 0))
    )
    d_projected = jnp.concatenate(
        [d_queries, d_kv, g_gate.reshape(num_rows, D_SSM), d_conv_in.reshape(num_rows, XBC)], axis=1
    ).astype(jnp.bfloat16)
    d_dt_low = d_dt_raw.reshape(num_rows, SSM_HEADS).astype(jnp.bfloat16)
    pad = jnp.zeros((num_rows, 128 - SSM_HEADS), jnp.bfloat16)
    grad_in = outer_total(normed, jnp.concatenate([d_projected, d_dt_low, pad], axis=1))
    share_in = chip_scatter(core_sums(grad_in.astype(jnp.bfloat16)))
    d_normed = times_rows(d_projected, full_in) + times_rows(d_dt_low, full_dt)
    d_hidden, d_gain1 = norm1_back(d_normed)
    d_hidden = d_hidden + d_second
    width = model_width // lax.axis_size("seq")
    in_width = share_gu.shape[1] // lax.axis_size("seq")
    total_gu = seq_scatter(lambda k: columns(share_gu, k, in_width))
    total_pair = seq_scatter(lambda k: columns(share_pair, k, width))
    pair_rows = total_pair.shape[0] // 2
    in_cols = d_projected.shape[1]
    total_in = seq_scatter(
        lambda k: jnp.concatenate(
            [columns(share_in[:, :in_cols], k, in_width), share_in[:, in_cols:]], axis=1
        )
    )
    summed_small = lax.psum(
        (jnp.stack([d_gain1, d_gain2]), g_conv, g_ssm, g_head_out + g_head_in),
        ("fsdp", "seq"),
    )
    return (
        result.reshape(num_seqs, span_len, model_width).astype(jnp.bfloat16),
        d_hidden.reshape(num_seqs, span_len, model_width),
        total_in[:, :in_width],
        total_in[:, in_width : in_width + SSM_HEADS],
        total_pair[pair_rows:],
        total_gu,
        total_pair[:pair_rows],
        summed_small[0],
        summed_small[1],
        summed_small[2],
        summed_small[3],
    )


def solution(mesh):
    placed = (
        P("fsdp", "seq", None),
        P("fsdp", "seq", None),
        P("fsdp", "seq"),
        P("fsdp", "seq"),
        P("fsdp", None),
        P("fsdp", "seq"),
        P("fsdp", "seq"),
        P("fsdp", "seq"),
        P(),
        P(),
        P(),
        P(),
    )
    return jax.shard_map(
        body,
        mesh=mesh,
        in_specs=placed,
        out_specs=(
            P("fsdp", "seq", None),
            P("fsdp", "seq", None),
            P("fsdp", "seq"),
            P("fsdp", None),
            P("fsdp", "seq"),
            P("fsdp", "seq"),
            P("fsdp", "seq"),
            P(),
            P(),
            P(),
            P(),
        ),
        check_vma=False,
    )
```

```python
import math
from functools import partial

import jax
import jax.numpy as jnp
from jax import lax
from jax.sharding import PartitionSpec as P

FF = 2048
HEADS = 8
KV_HEADS = 2
HEAD_DIM = 64
SSM_HEADS = 24
SSM_DIM = 64
STATE = 128
CONV = 4
D_SSM = 1536
XBC = 1792


EPSILON = 1e-05
PRECISE = lax.Precision.HIGHEST


def passed_along(block, axis, distance):
    devices = range(lax.axis_size(axis))
    route = [(i - distance, i) for i in devices if i - distance in devices]
    return lax.ppermute(block, axis, route)


def entering_states(decay, state, direction):
    count = lax.axis_size("seq")
    rank = lax.axis_index("seq")
    if direction < 0:
        rank = count - 1 - rank
    decay = jnp.where(rank == 0, 1.0, passed_along(decay, "seq", direction))
    state = passed_along(state.astype(jnp.bfloat16), "seq", direction).astype(jnp.float32)
    reach = 1
    while reach < count - 1:
        earlier = passed_along(decay, "seq", direction * reach)
        lower = passed_along(state.astype(jnp.bfloat16), "seq", direction * reach)
        joined = decay[:, :, None, None] * lower.astype(jnp.float32) + state
        state = jnp.where(rank >= reach, joined, state)
        decay = jnp.where(rank >= reach, decay * earlier, decay)
        reach *= 2
    return state


def row_scatter(grad):
    return lax.psum_scatter(grad, "fsdp", scatter_dimension=0, tiled=True)


def rms_norm(values, gain):
    return values * lax.rsqrt(jnp.mean(values * values, axis=-1, keepdims=True) + EPSILON) * gain


def swiglu(paired):
    return jax.nn.silu(paired[:, :FF]) * paired[:, FF:]


def times_rows(left, weight):
    return lax.dot_general(
        left, weight, (((1,), (1,)), ((), ())), preferred_element_type=jnp.float32
    )


def outer_total(left, right):
    return lax.dot_general(
        left, right, (((0,), (0,)), ((), ())), preferred_element_type=jnp.float32
    )


def seq_gather(block, axis):
    count, place = lax.axis_size("seq"), lax.axis_index("seq")
    size = block.shape[axis]
    shape = list(block.shape)
    shape[axis] *= count
    whole = jnp.zeros(shape, block.dtype)
    whole = lax.dynamic_update_slice_in_dim(whole, block, place * size, axis)
    for hop in range(1, count):
        route = [(d, (d + hop) % count) for d in range(count)]
        came = lax.ppermute(block, "seq", route)
        source = lax.rem(place - hop + count, count)
        whole = lax.dynamic_update_slice_in_dim(whole, came, source * size, axis)
    return whole


def seq_scatter(pick):
    count, place = lax.axis_size("seq"), lax.axis_index("seq")
    total = pick(place).astype(jnp.float32)
    for hop in range(1, count):
        route = [(d, (d + hop) % count) for d in range(count)]
        target = lax.rem(place + hop, count)
        total = total + lax.ppermute(pick(target), "seq", route).astype(jnp.float32)
    return total


def columns(array, place, width):
    return lax.dynamic_slice_in_dim(array, place * width, width, 1)


def per_channel(array):
    return jnp.repeat(array, SSM_DIM, axis=-1)


def conv_pieces(extended, conv_params, dt_raw, head_params, valid, chunk):
    num, length = dt_raw.shape[:2]
    summed = conv_params[CONV] + jnp.zeros((num, length, XBC), jnp.float32)
    for lagged in range(CONV):
        offset = CONV - 1 - lagged
        summed = (
            summed
            + conv_params[lagged]
            * extended[:, offset : offset + length, :]
            * valid[lagged][..., None]
        )
    activated = jax.nn.silu(summed).reshape(num, length // chunk, chunk, XBC)
    inputs = activated[..., :D_SSM]
    b_proj = activated[..., D_SSM : D_SSM + STATE]
    c_proj = activated[..., D_SSM + STATE :]
    step_size = jax.nn.softplus(dt_raw + head_params[1])
    step_size = step_size.reshape(num, length // chunk, chunk, SSM_HEADS)
    lower = jnp.tril(jnp.ones((chunk, chunk), jnp.float32))
    cumul = jnp.einsum(
        "tr,scrh->scth", lower, -jnp.exp(head_params[0]) * step_size, precision=PRECISE
    )
    return (inputs, b_proj, c_proj, step_size, cumul)


def block_summary(inputs, b_proj, step_size, cumul, tail_mask, alive):
    final = cumul[:, :, -1, :]
    decay = jnp.exp(final) * alive[..., None]
    weights = jnp.exp(final[:, :, None, :] - cumul) * step_size * tail_mask[..., None]
    state = jnp.einsum(
        "scpe,scpn->scen", per_channel(weights) * inputs, b_proj, preferred_element_type=jnp.float32
    )
    num, chunks = state.shape[:2]
    state = state.reshape(num, chunks, SSM_HEADS, SSM_DIM, STATE)
    reach = jnp.ones_like(decay[:, 0])
    carried = jnp.zeros_like(state[:, 0])
    reaches, carries = [], []
    for k in range(chunks):
        reaches.append(reach)
        carries.append(carried)
        carried = decay[:, k][:, :, None, None] * carried + state[:, k]
        reach = reach * decay[:, k]
    return (reach, carried, jnp.stack(reaches, 1), jnp.stack(carries, 1))


def block_output(
    inputs,
    b_proj,
    c_proj,
    step_size,
    cumul,
    head_params,
    reaches,
    carries,
    entering,
    gate_in,
    ssm_gain,
    inner_mask,
    carry_mask,
):
    num, chunks, chunk = inputs.shape[:3]
    gram = jnp.einsum("sctn,scrn->sctr", c_proj, b_proj, preferred_element_type=jnp.float32)
    cumul_h = jnp.swapaxes(cumul, 2, 3)
    step_h = jnp.swapaxes(step_size, 2, 3)
    spread = cumul_h[..., :, None] - cumul_h[..., None, :]
    decays = jnp.exp(jnp.where(inner_mask[:, :, None], spread, -1e30))
    weights = decays * (gram[:, :, None] * step_h[..., None, :])
    heads = inputs.reshape(num, chunks, chunk, SSM_HEADS, SSM_DIM)
    within = jnp.einsum(
        "schtr,scrhd->scthd", weights, heads, preferred_element_type=jnp.float32
    ).reshape(inputs.shape)
    entry = jnp.exp(cumul) * carry_mask[..., None]
    states = carries + reaches[..., None, None] * entering[:, None]
    states = states.reshape(num, chunks, D_SSM, STATE)
    incoming = per_channel(entry) * jnp.einsum(
        "scen,sctn->scte", states, c_proj, preferred_element_type=jnp.float32
    )
    output = within + incoming + per_channel(head_params[2]) * inputs
    output = output.reshape(num, chunks * chunk, D_SSM) * jax.nn.silu(gate_in)
    return rms_norm(output, ssm_gain)


def body(
    tokens,
    cotangent,
    doc_start,
    w_in,
    w_dt,
    w_out,
    w_gate_up,
    w_down,
    norm_gains,
    conv_params,
    ssm_gain,
    head_params,
):
    num_seqs, span_len, model_width = tokens.shape
    num_rows = num_seqs * span_len
    block_start = lax.axis_index("seq") * span_len
    q_width = HEADS * HEAD_DIM
    kv_width = KV_HEADS * HEAD_DIM
    head_share = HEADS // KV_HEADS
    att_scale = HEAD_DIM ** (-0.5)
    rim_len = CONV - 1
    chunk = math.gcd(span_len, 128)
    chunks = span_len // chunk
    base_col = q_width + 2 * kv_width
    cols_in, cols_out, cols_gu, cols_down = (
        seq_gather(w_in, 1),
        seq_gather(w_out, 1),
        seq_gather(w_gate_up, 1),
        seq_gather(w_down, 1),
    )
    full_in, full_dt, full_out, full_gu, full_down = (
        lax.all_gather(cols_in, "fsdp", axis=0, tiled=True),
        lax.all_gather(w_dt, "fsdp", axis=0, tiled=True),
        lax.all_gather(cols_out, "fsdp", axis=0, tiled=True),
        lax.all_gather(cols_gu, "fsdp", axis=0, tiled=True),
        lax.all_gather(cols_down, "fsdp", axis=0, tiled=True),
    )
    hidden = tokens.reshape(num_rows, model_width).astype(jnp.float32)
    normed_f, norm1_back = jax.vjp(rms_norm, hidden, norm_gains[0])
    normed = normed_f.astype(jnp.bfloat16)
    projected = jnp.dot(normed, full_in, preferred_element_type=jnp.float32).astype(jnp.bfloat16)
    dt_raw = jnp.dot(normed, full_dt, preferred_element_type=jnp.float32)
    queries = projected[:, :q_width].reshape(num_rows, KV_HEADS, head_share, HEAD_DIM)
    kv_all = seq_gather(projected[:, q_width:base_col], 0)
    total_keys = kv_all.shape[0]
    keys_all = kv_all[:, :kv_width].reshape(total_keys, KV_HEADS, HEAD_DIM)
    values_all = kv_all[:, kv_width:].reshape(total_keys, KV_HEADS, HEAD_DIM)
    row_index = jnp.arange(num_rows, dtype=jnp.int32)
    q_seq = row_index // span_len
    q_pos = block_start + row_index % span_len
    row_starts = doc_start.reshape(num_rows)
    key_index = jnp.arange(total_keys, dtype=jnp.int32)
    key_within = key_index % num_rows
    k_seq = key_within // span_len
    k_pos = key_index // num_rows * span_len + key_within % span_len
    allowed = (
        (k_seq[None, :] == q_seq[:, None])
        & (k_pos[None, :] <= q_pos[:, None])
        & (k_pos[None, :] >= row_starts[:, None])
    )
    scores = (
        jnp.einsum("tkgd,ckd->kgtc", queries, keys_all, preferred_element_type=jnp.float32)
        * att_scale
    )
    scores = jnp.where(allowed, scores, -1e30)
    row_max = jnp.max(scores, axis=-1, keepdims=True)
    shifted = jnp.exp(scores - row_max)
    attn_probs = shifted / jnp.sum(shifted, axis=-1, keepdims=True)
    probs_low = attn_probs.astype(jnp.bfloat16)
    attended = (
        jnp.einsum("kgtc,ckd->tkgd", probs_low, values_all, preferred_element_type=jnp.float32)
        .reshape(num_rows, q_width)
        .astype(jnp.bfloat16)
    )
    gate_in = (
        projected[:, base_col : base_col + D_SSM]
        .astype(jnp.float32)
        .reshape(num_seqs, span_len, D_SSM)
    )
    conv_in = projected[:, base_col + D_SSM :].reshape(num_seqs, span_len, XBC)
    before = passed_along(conv_in[:, span_len - rim_len :, :], "seq", 1)
    extended = jnp.concatenate([before, conv_in], axis=1).astype(jnp.float32)
    positions = block_start + jnp.arange(span_len, dtype=jnp.int32)
    valid = jnp.stack([positions[None, :] - lagged >= doc_start for lagged in range(CONV)]).astype(
        jnp.float32
    )
    pieces, pieces_back = jax.vjp(
        partial(conv_pieces, valid=valid, chunk=chunk),
        extended,
        conv_params,
        dt_raw.reshape(num_seqs, span_len, SSM_HEADS),
        head_params,
    )
    inputs, b_proj, c_proj, step_size, cumul = pieces
    starts = doc_start.reshape(num_seqs, chunks, chunk)
    places = positions.reshape(chunks, chunk)
    chunk_start = places[:, :1]
    tail_mask = (places >= starts[..., -1:]).astype(jnp.float32)
    alive_mask = (starts[..., -1] < places[:, 0]).astype(jnp.float32)
    summary, summary_back = jax.vjp(
        partial(block_summary, tail_mask=tail_mask, alive=alive_mask),
        inputs,
        b_proj,
        step_size,
        cumul,
    )
    entering = entering_states(summary[0], summary[1], 1)
    inner_mask = (places[:, None, :] <= places[:, :, None]) & (
        places[:, None, :] >= starts[..., None]
    )
    carry_mask = (starts < chunk_start).astype(jnp.float32)
    mamba_f, output_back = jax.vjp(
        partial(block_output, inner_mask=inner_mask, carry_mask=carry_mask),
        inputs,
        b_proj,
        c_proj,
        step_size,
        cumul,
        head_params,
        summary[2],
        summary[3],
        entering,
        gate_in,
        ssm_gain,
    )
    mamba_low = mamba_f.reshape(num_rows, D_SSM).astype(jnp.bfloat16)
    mixed_in = jnp.concatenate([attended, mamba_low], axis=1)
    second = hidden + jnp.dot(mixed_in, full_out, preferred_element_type=jnp.float32)
    normed2_f, norm2_back = jax.vjp(rms_norm, second, norm_gains[1])
    normed2 = normed2_f.astype(jnp.bfloat16)
    paired = jnp.dot(normed2, full_gu, preferred_element_type=jnp.float32)
    activ_f, activ_back = jax.vjp(swiglu, paired)
    activ = activ_f.astype(jnp.bfloat16)
    result = second + jnp.dot(activ, full_down, preferred_element_type=jnp.float32)
    upstream = cotangent.reshape(num_rows, model_width)
    grad_down = outer_total(activ, upstream)
    d_activ = times_rows(upstream, full_down)
    d_paired = activ_back(d_activ)[0].astype(jnp.bfloat16)
    grad_gu = outer_total(normed2, d_paired)
    grad_gu, grad_down, d_paired = lax.optimization_barrier(
        (grad_gu.astype(jnp.bfloat16), grad_down.astype(jnp.bfloat16), d_paired)
    )
    share_gu = row_scatter(grad_gu)
    d_normed2 = times_rows(d_paired, full_gu)
    d_second, d_gain2 = norm2_back(d_normed2)
    d_second = d_second + upstream.astype(jnp.float32)
    d_mixed = d_second.astype(jnp.bfloat16)
    grad_out = outer_total(mixed_in, d_mixed)
    grad_pair = jnp.concatenate([grad_down, grad_out.astype(jnp.bfloat16)], axis=1)
    grad_pair, d_mixed = lax.optimization_barrier((grad_pair, d_mixed))
    share_pair = row_scatter(grad_pair)
    d_mixed_in = times_rows(d_mixed, full_out)
    d_attended = (
        d_mixed_in[:, :q_width]
        .astype(jnp.bfloat16)
        .reshape(num_rows, KV_HEADS, head_share, HEAD_DIM)
    )
    d_mamba = d_mixed_in[:, q_width:].reshape(num_seqs, span_len, D_SSM)
    d_probs = jnp.einsum(
        "tkgd,ckd->kgtc", d_attended, values_all, preferred_element_type=jnp.float32
    )
    centre = jnp.sum(attn_probs * d_probs, axis=-1, keepdims=True)
    d_scores = (attn_probs * (d_probs - centre)).astype(jnp.bfloat16)
    d_queries = (
        jnp.einsum("kgtc,ckd->tkgd", d_scores, keys_all, preferred_element_type=jnp.float32)
        * att_scale
    ).reshape(num_rows, q_width)
    d_keys = (
        jnp.einsum("kgtc,tkgd->ckd", d_scores, queries, preferred_element_type=jnp.float32)
        * att_scale
    )
    d_values = jnp.einsum(
        "kgtc,tkgd->ckd", probs_low, d_attended, preferred_element_type=jnp.float32
    )
    d_kv_all = jnp.concatenate(
        [d_keys.reshape(total_keys, kv_width), d_values.reshape(total_keys, kv_width)], axis=1
    ).astype(jnp.bfloat16)
    d_kv = seq_scatter(lambda k: lax.dynamic_slice_in_dim(d_kv_all, k * num_rows, num_rows, 0))
    g_inputs, g_bproj, g_cproj, g_step, g_cumul, g_head_out, g_reaches, g_carries, *g_rest = (
        output_back(d_mamba)
    )
    g_entering, g_gate, g_ssm = g_rest
    state_grad = entering_states(summary[0], g_entering, -1)
    d_decay = jnp.sum(state_grad * entering, axis=(2, 3))
    s_inputs, s_bproj, s_step, s_cumul = summary_back(
        (d_decay, state_grad, g_reaches, g_carries)
    )
    d_extended, g_conv, d_dt_raw, g_head_in = pieces_back(
        (g_inputs + s_inputs, g_bproj + s_bproj, g_cproj, g_step + s_step, g_cumul + s_cumul)
    )
    from_next = passed_along(d_extended[:, :rim_len, :], "seq", -1)
    d_conv_in = d_extended[:, rim_len:, :] + jnp.pad(
        from_next, ((0, 0), (span_len - rim_len, 0), (0, 0))
    )
    d_projected = jnp.concatenate(
        [d_queries, d_kv, g_gate.reshape(num_rows, D_SSM), d_conv_in.reshape(num_rows, XBC)], axis=1
    ).astype(jnp.bfloat16)
    d_dt_low = d_dt_raw.reshape(num_rows, SSM_HEADS).astype(jnp.bfloat16)
    pad = jnp.zeros((num_rows, 128 - SSM_HEADS), jnp.bfloat16)
    grad_in = outer_total(normed, jnp.concatenate([d_projected, d_dt_low, pad], axis=1))
    share_in = row_scatter(grad_in.astype(jnp.bfloat16))
    d_normed = times_rows(d_projected, full_in) + times_rows(d_dt_low, full_dt)
    d_hidden, d_gain1 = norm1_back(d_normed)
    d_hidden = d_hidden + d_second
    width = model_width // lax.axis_size("seq")
    in_width = share_gu.shape[1] // lax.axis_size("seq")
    total_gu = seq_scatter(lambda k: columns(share_gu, k, in_width))
    total_pair = seq_scatter(
        lambda k: jnp.concatenate(
            [
                columns(share_pair[:, :model_width], k, width),
                columns(share_pair[:, model_width:], k, width),
            ],
            axis=1,
        )
    )
    in_cols = d_projected.shape[1]
    total_in = seq_scatter(
        lambda k: jnp.concatenate(
            [columns(share_in[:, :in_cols], k, in_width), share_in[:, in_cols:]], axis=1
        )
    )
    summed_small = lax.psum(
        (jnp.stack([d_gain1, d_gain2]), g_conv, g_ssm, g_head_out + g_head_in),
        ("fsdp", "seq"),
    )
    return (
        result.reshape(num_seqs, span_len, model_width).astype(jnp.bfloat16),
        d_hidden.reshape(num_seqs, span_len, model_width),
        total_in[:, :in_width],
        total_in[:, in_width : in_width + SSM_HEADS],
        total_pair[:, width:],
        total_gu,
        total_pair[:, :width],
        summed_small[0],
        summed_small[1],
        summed_small[2],
        summed_small[3],
    )


def solution(mesh):
    placed = (
        P("fsdp", "seq", None),
        P("fsdp", "seq", None),
        P("fsdp", "seq"),
        P("fsdp", "seq"),
        P("fsdp", None),
        P("fsdp", "seq"),
        P("fsdp", "seq"),
        P("fsdp", "seq"),
        P(),
        P(),
        P(),
        P(),
    )
    return jax.shard_map(
        body,
        mesh=mesh,
        in_specs=placed,
        out_specs=(
            P("fsdp", "seq", None),
            P("fsdp", "seq", None),
            P("fsdp", "seq"),
            P("fsdp", None),
            P("fsdp", "seq"),
            P("fsdp", "seq"),
            P("fsdp", "seq"),
            P(),
            P(),
            P(),
            P(),
        ),
        check_vma=False,
    )
```
